512 devices in a mesh: seq: 16 (over z, core), fsdp: 32 (over y, x).
Axes of the slice: x: 4, y: 8, z: 8, core: 2. Of those that a mesh axis runs over, the one named last changes fastest.
Arguments:
- latents: bfloat16 [32, 2048, 2432], P('fsdp', 'seq'), may hold values from -6 to 6
- noise: bfloat16 [32, 2048, 2432], P('fsdp', 'seq'), may hold values from -6 to 6
- timesteps: int32 [32], P('fsdp'), may hold values from 1 to 999
- time_weight: bfloat16 [256, 4864], P(None, 'fsdp'), may hold values from -0.375 to 0.375
- qkv_weight: bfloat16 [2432, 3, 2048], P(None, None, 'seq'), may hold values from -0.125 to 0.125
- cached_targets: bfloat16 [16384, 2048], P('fsdp', 'seq'), may hold values from -6 to 6
- cache_owner: int32 [16384, 1], P('fsdp'), may hold values from 0 to 31; in each aligned block of 512 rows (0 to 511, 512 to 1023, ...) at most 32 rows name the same one
- cache_pos: int32 [16384], P('fsdp'), may hold values from 0 to 2047
Outputs:
- critic_grad: bfloat16 [32, 2048, 2048], P('fsdp', None, 'seq')
The draws below stay inside these ranges and needn't reach their ends.
Inputs may be any that keep to these rules, and one draw needn't show every extreme that they name: `cache_owner`: in the rows of one index of fsdp (512 aligned rows) no sample is named more than 32 times, a bound that some block reaches.
All inputs are finite; a program needn't handle non-finite values.
Results may differ from the reference program's by a relative error of at most 0.012.
Values may be sent and summed in bfloat16 or wider, within the bound.
No kernel may reach another device: no remote copies, remote signals or barrier semaphores. Data moves between devices by JAX's collectives and lax.ppermute only.
A program may use at most 64 MiB of HBM per device.

```python
import math
import jax
import jax.numpy as jnp
import numpy as np
from jax import lax

D = 2432
HEAD_DIM = 64
FREQ = 256
C_DEV = 512
HEADS = 32
HD = 2048
LENGTH = 2048
SAMPLES = 32
CACHE_ROWS = 16384
SLOT = 32


def plant(array, stream_key, smallest, top_value):
    longest = array.shape.index(max(array.shape))
    spots = []
    for shift in (0, 1):
        where = [jax.random.randint(jax.random.fold_in(stream_key, axis), (), 0, length) for axis, length in enumerate(array.shape)]
        where[longest] = (where[longest] + shift) % array.shape[longest]
        spots.append(tuple(where))
    return array.at[spots[0]].set(smallest).at[spots[1]].set(top_value)


def block_levels(stream_key, extent, split, least, top_value):
    factor_of, own = 1.0, jax.random.fold_in(stream_key, 6)
    for position, parts in split:
        heights = jnp.exp(jax.random.uniform(jax.random.fold_in(own, position), (parts,), jnp.float32, least / len(split), top_value / len(split)))
        factor_of = factor_of * jnp.repeat(heights, extent[position] // parts).reshape([-1 if axis == position else 1 for axis in range(len(extent))])
    return factor_of


def routed_block(stream_key, own, number, rows, number_of, top, most, lean):
    ranking = jax.random.permutation(stream_key, number_of)
    packed, common = portions_of(number_of, rows * top, most, lean, True), portions_of(number_of, rows * top, most, lean, False)
    places = jnp.arange(number_of)

    def named(lengths, offset_by):
        used = int((lengths > 0).sum())
        fixed = max(1, used // 4)
        passed = fixed + (places - fixed + offset_by * (used - fixed)) % max(1, number_of - fixed)
        return jnp.zeros((number_of,), jnp.int32).at[ranking[jnp.where(places < fixed, places, passed)]].set(jnp.asarray(lengths, jnp.int32))

    lengths = jnp.where(number % 4 == 0, named(packed, number // 4), named(common, number - number // 4 - 1))
    mixed = jax.random.permutation(jax.random.fold_in(own, 3), number_of)
    giver, taker = mixed[0:number_of // 2 * 2:2], mixed[1:number_of // 2 * 2:2]
    room = jnp.minimum(lengths[giver] - 1, most - lengths[taker]) // 2
    room = jnp.where((giver == ranking[0]) | (taker == ranking[0]) | (lengths[taker] == 0), 0, jnp.maximum(room, 0))
    passed = jax.random.randint(jax.random.fold_in(own, 4), (number_of // 2,), 0, 1 << 20) % (room + 1)
    lengths = lengths.at[giver].add(-passed).at[taker].add(passed)
    items = jnp.searchsorted(jnp.cumsum(lengths), jnp.arange(rows * top), side="right").astype(jnp.int32)
    table = items.reshape(top, rows).T
    table = table[jax.random.permutation(jax.random.fold_in(own, 1), rows)]
    offset_by = jax.random.randint(jax.random.fold_in(own, 2), (rows, 1), 0, top)
    return jnp.take_along_axis(table, (jnp.arange(top)[None, :] + offset_by) % top, axis=1)


def portions_of(count, total, bound, slope, full):
    portions = [(1 << 20) // math.isqrt(standing ** slope) + 1 for standing in range(1, count + 1)]
    largest = bound if full else min(bound, max(-(-total // count), total * portions[0] // sum(portions)))
    least = 1 if total - largest >= count - 1 else 0
    counts, spare = [largest] + [least] * (count - 1), total - largest - least * (count - 1)
    while spare > 0:
        free = [i for i in range(1, count) if counts[i] < largest] or [i for i in range(1, count) if counts[i] < bound]
        whole, budget = sum([portions[i] for i in free]), spare
        for i in free:
            more = min(bound - counts[i], max(1, budget * portions[i] // whole), spare)
            counts[i] = counts[i] + more
            spare = spare - more
    return np.array(counts)


def scatter_about(stream_key, shape, deviation, limit, cuts=(), held_as=jnp.bfloat16):
    entries = deviation * jax.random.normal(stream_key, shape, jnp.float32)
    if cuts:
        entries = entries * block_levels(stream_key, shape, cuts, -0.22, 0.18)
    return jnp.clip(entries, -limit, limit).astype(held_as)


def setup_inputs(seed: int = 0) -> dict:
    seeds = jax.random.split(jax.random.key(seed), 9)
    latents = scatter_about(seeds[0], (SAMPLES, LENGTH, D), 1.0, 6.0, ((0, 32), (1, 16)))
    noise = scatter_about(seeds[1], (SAMPLES, LENGTH, D), 1.0, 6.0, ((0, 32), (1, 16)))
    timesteps = plant(jax.random.randint(seeds[2], (SAMPLES,), 1, 1000), jax.random.fold_in(seeds[2], 1), 1, 999).astype(jnp.int32)
    time_weight = scatter_about(seeds[3], (FREQ, 2 * D), FREQ ** -0.5, 0.375, ((1, 32),))
    qkv_weight = scatter_about(seeds[4], (D, 3, HD), D ** -0.5, 0.125, ((2, 16),))
    cached_targets = scatter_about(seeds[5], (CACHE_ROWS, HD), 1.0, 6.0, ((0, 32), (1, 16)))
    cache_owner_keys = jax.random.split(jax.random.fold_in(seeds[6], 1), CACHE_ROWS // C_DEV)
    cache_owner_turns = jax.random.permutation(jax.random.fold_in(seeds[6], 3), CACHE_ROWS // C_DEV)
    cache_owner = jax.vmap(lambda own, number: routed_block(jax.random.fold_in(seeds[6], 2), own, number, C_DEV, SAMPLES, 1, SLOT, 2))(cache_owner_keys, cache_owner_turns).reshape((CACHE_ROWS, 1))
    cache_pos = plant(jax.random.randint(seeds[7], (CACHE_ROWS,), 0, LENGTH), jax.random.fold_in(seeds[7], 1), 0, LENGTH - 1).astype(jnp.int32)
    return dict(latents=latents, noise=noise, timesteps=timesteps, time_weight=time_weight, qkv_weight=qkv_weight, cached_targets=cached_targets, cache_owner=cache_owner, cache_pos=cache_pos)


def embed_times(stamps):
    half = FREQ // 2
    steps = jnp.arange(half, dtype=jnp.float32)
    freqs = jnp.exp(-math.log(10000.0) * steps / half)
    angles = stamps.astype(jnp.float32)[:, None] * freqs[None, :]
    raw = jnp.concatenate([jnp.cos(angles), jnp.sin(angles)], axis=1)
    return jax.nn.silu(raw).astype(jnp.bfloat16)

def reference(latents, noise, timesteps, time_weight, qkv_weight, cached_targets, cache_owner, cache_pos):
    embed = embed_times(timesteps)
    modulation = jnp.dot(embed, time_weight, preferred_element_type=jnp.float32)
    shift = modulation[:, :D][:, None, :]
    scale = modulation[:, D:][:, None, :]
    sigma = (timesteps.astype(jnp.float32) / 1000.0)[:, None, None]
    noised = (1.0 - sigma) * latents.astype(jnp.float32) + sigma * noise.astype(jnp.float32)
    center = lax.optimization_barrier(jnp.mean(noised, axis=2, keepdims=True))
    spread = lax.optimization_barrier(jnp.mean((noised - center) ** 2, axis=2, keepdims=True))
    normed = (noised - center) / jnp.sqrt(spread + 1e-06)
    modulated = (normed * (1.0 + scale) + shift).astype(jnp.bfloat16)
    flat_weight = qkv_weight.reshape(D, 3 * HD)

    def one_sample(rows):
        qkv = jnp.dot(rows, flat_weight, preferred_element_type=jnp.float32).astype(jnp.bfloat16)
        qkv = qkv.reshape(LENGTH, 3, HEADS, HEAD_DIM).astype(jnp.float32)
        scores = jnp.einsum('qhd,khd->hqk', qkv[:, 0], qkv[:, 1]) / math.sqrt(HEAD_DIM)
        probs = jax.nn.softmax(scores, axis=-1).astype(jnp.bfloat16)
        attended = jnp.einsum('hqk,khd->qhd', probs.astype(jnp.float32), qkv[:, 2])
        return attended.reshape(LENGTH, HD)
    attended = lax.map(one_sample, modulated)
    index = cache_owner[:, 0].astype(jnp.int32) * LENGTH + cache_pos.astype(jnp.int32)
    target_sum = jax.ops.segment_sum(cached_targets.astype(jnp.float32), index, SAMPLES * LENGTH)
    count = jax.ops.segment_sum(jnp.ones((CACHE_ROWS,), jnp.float32), index, SAMPLES * LENGTH)
    target_sum = target_sum.reshape(SAMPLES, LENGTH, HD)
    count = count.reshape(SAMPLES, LENGTH, 1)
    return (count * attended - target_sum).astype(jnp.bfloat16)
```

```python
import functools
import math

import jax
import jax.numpy as jnp
from jax import lax
from jax.experimental import pallas as pl
from jax.experimental.pallas import tpu as pltpu
from jax.sharding import PartitionSpec as P

HEAD_DIM = 64
FREQ = 256
F32 = jnp.float32
BF16 = jnp.bfloat16


def embed_times(stamps):
    half = FREQ // 2
    steps = jnp.arange(half, dtype=F32)
    freqs = jnp.exp(-math.log(10000.0) * steps / half)
    angles = stamps.astype(F32)[:, None] * freqs[None, :]
    raw = jnp.concatenate([jnp.cos(angles), jnp.sin(angles)], axis=1)
    return jax.nn.silu(raw).astype(BF16)


def norm_kernel(stamp_ref, latents_ref, noise_ref, out_ref):
    sigma = stamp_ref[0].astype(F32) / 1000.0
    noised = (1.0 - sigma) * latents_ref[...].astype(F32) + sigma * noise_ref[...].astype(F32)
    center = jnp.mean(noised, axis=1, keepdims=True)
    shifted = noised - center
    spread = jnp.mean(shifted * shifted, axis=1, keepdims=True)
    out_ref[...] = (shifted / jnp.sqrt(spread + 1e-06)).astype(BF16)


def normalize(timesteps, latents, noise):
    rows, dmodel = latents.shape
    block = 32
    spec = pl.BlockSpec((block, dmodel), lambda i: (i, 0))
    return pl.pallas_call(
        norm_kernel,
        grid=(rows // block,),
        in_specs=[pl.BlockSpec(memory_space=pltpu.SMEM), spec, spec],
        out_specs=spec,
        out_shape=jax.ShapeDtypeStruct((rows, dmodel), BF16),
        name="normalize",
    )(timesteps, latents, noise)


def pack_rows(targets, owners, places, timesteps, samples):
    crows, width = targets.shape
    slots = 32
    sample_ids = jnp.arange(samples, dtype=jnp.int32)
    owned = owners[:, None] == sample_ids[None, :]
    order = jnp.arange(crows, dtype=jnp.int32)
    strict = (order[:, None] > order[None, :]).astype(BF16)
    before = jnp.dot(strict, owned.astype(BF16), preferred_element_type=F32)
    rank = jnp.sum(jnp.where(owned, before, 0.0), axis=1).astype(jnp.int32)
    slot = owners * slots + rank
    select = (jnp.arange(samples * slots, dtype=jnp.int32)[:, None] == slot[None, :]).astype(BF16)
    rows = jnp.dot(select, targets, preferred_element_type=F32).astype(BF16)
    ranked = rank[:, None] == jnp.arange(slots, dtype=jnp.int32)[None, :]
    high = (places // 64 + 1).astype(F32)[:, None]
    low = (places % 64).astype(F32)[:, None]
    coded = jnp.concatenate([jnp.where(ranked, high, 0.0), jnp.where(ranked, low, 0.0)], axis=1)
    where_to = jnp.einsum(
        "rs,rc->sc", owned.astype(BF16), coded.astype(BF16), preferred_element_type=F32
    )
    stamp = jnp.broadcast_to(
        jnp.concatenate([timesteps // 32, timesteps % 32]).astype(F32)[None, :], (samples, 2)
    )
    extra = jnp.concatenate(
        [where_to, stamp, jnp.zeros((samples, width - 2 * slots - 2), F32)], axis=1
    ).astype(BF16)
    extra = jnp.broadcast_to(extra[:, None, :], (samples, 16, width))
    return jnp.concatenate([rows.reshape(samples, slots, width), extra], axis=1)


def attend_kernel(
    x_ref, weight_ref, bias_ref, column_ref, row_ref, target_ref, out_ref,
    key_ref, first_ref, second_ref, query_ref, diff_ref,
):
    step = pl.program_id(0)
    block = x_ref.shape[0]
    slots, width = query_ref.shape
    length = key_ref.shape[0]
    here = pl.ds(pl.multiple_of(step * block, block), block)
    qkv = jnp.dot(x_ref[...], weight_ref[...], preferred_element_type=F32) + bias_ref[...]
    qkv = qkv.astype(BF16)
    left = lax.broadcasted_iota(jnp.int32, (block, width), 1) < HEAD_DIM
    one = jnp.ones((block, width), BF16)
    key_ref[here, :] = qkv[:, width : 2 * width]
    value = qkv[:, 2 * width :]
    first_ref[here, :] = jnp.where(left, value, one)
    second_ref[here, :] = jnp.where(left, one, value)
    spots = lax.broadcasted_iota(jnp.int32, (slots, block), 1) + step * block
    pick = (column_ref[...] == spots).astype(F32).astype(BF16)
    picked = jnp.dot(pick, qkv[:, :width], preferred_element_type=F32)

    @pl.when(step == 0)
    def _():
        query_ref[...] = picked

    @pl.when(step > 0)
    def _():
        query_ref[...] += picked

    @pl.when(step == pl.num_programs(0) - 1)
    def _():
        factor = math.log2(math.e) / math.sqrt(HEAD_DIM)
        part = 256
        half = lax.broadcasted_iota(jnp.int32, (part, width), 1) < HEAD_DIM
        for start in range(0, slots, part):
            query = query_ref[start : start + part, :]
            outs = []
            for keep, value_ref in ((half, first_ref), (~half, second_ref)):
                mine = jnp.where(keep, query, 0.0).astype(BF16)
                scores = lax.dot_general(
                    mine, key_ref[...], (((1,), (1,)), ((), ())), preferred_element_type=F32
                )
                top = jnp.max(scores, axis=1, keepdims=True)
                probs = jnp.exp2((scores - top) * factor).astype(BF16)
                mixed = jnp.dot(probs, value_ref[...], preferred_element_type=F32)
                outs.append(mixed / pltpu.roll(mixed, HEAD_DIM, 1))
            attended = jnp.where(half, outs[0], outs[1])
            target = target_ref[start : start + part, :].astype(F32)
            diff_ref[start : start + part, :] = (attended - target).astype(BF16)
        for start in range(0, length, part):
            spots = lax.broadcasted_iota(jnp.int32, (part, slots), 0) + start
            spread = (row_ref[...] == spots).astype(F32).astype(BF16)
            out_ref[start : start + part, :] = jnp.dot(
                spread, diff_ref[...], preferred_element_type=F32
            ).astype(BF16)


def attend(tokens, weight, bias, spots, targets):
    length, dmodel = tokens.shape
    slots, width = targets.shape
    block = 256
    whole = lambda shape: pl.BlockSpec(shape, lambda i: (0, 0))
    return pl.pallas_call(
        attend_kernel,
        grid=(length // block,),
        in_specs=[
            pl.BlockSpec((block, dmodel), lambda i: (i, 0)),
            whole((dmodel, 3 * width)),
            whole((1, 3 * width)),
            whole((slots, 1)),
            whole((1, slots)),
            whole((slots, width)),
        ],
        out_specs=whole((length, width)),
        out_shape=jax.ShapeDtypeStruct((length, width), BF16),
        scratch_shapes=[
            pltpu.VMEM((length, width), BF16),
            pltpu.VMEM((length, width), BF16),
            pltpu.VMEM((length, width), BF16),
            pltpu.VMEM((slots, width), F32),
            pltpu.VMEM((slots, width), BF16),
        ],
        compiler_params=pltpu.CompilerParams(vmem_limit_bytes=48 * 1024 * 1024),
        name="attend",
    )(tokens, weight, bias, spots.reshape(slots, 1), spots.reshape(1, slots), targets)


def shards(
    latents, noise, timesteps, time_weight, qkv_weight, cached_targets, cache_owner, cache_pos
):
    dmodel = latents.shape[2]
    width = qkv_weight.shape[2]
    samples = lax.axis_size("fsdp")
    slots = 32
    normed = normalize(timesteps, latents[0], noise[0])
    tokens = lax.all_gather(normed, "seq", axis=0, tiled=True)
    sent = pack_rows(cached_targets, cache_owner[:, 0], cache_pos, timesteps, samples)
    got = lax.all_to_all(sent, "fsdp", 0, 0, tiled=True)
    targets = got[:, :slots].reshape(samples * slots, width)
    extra = got[:, slots].astype(F32)
    high, low = extra[:, :slots], extra[:, slots : 2 * slots]
    spots = jnp.where(high > 0.5, (high - 1.0) * 64.0 + low, -1.0).astype(jnp.int32)
    stamps = (extra[:, 2 * slots] * 32.0 + extra[:, 2 * slots + 1]).astype(jnp.int32)
    part = jnp.dot(embed_times(stamps), time_weight, preferred_element_type=F32)
    modulation = lax.all_to_all(part, "fsdp", 0, 0, tiled=True).reshape(2 * dmodel)
    shift = modulation[:dmodel]
    scale = modulation[dmodel:]
    flat_weight = qkv_weight.reshape(dmodel, 3 * width).astype(F32)
    weight = ((1.0 + scale)[:, None] * flat_weight).astype(BF16)
    bias = jnp.sum(shift[:, None] * flat_weight, axis=0, keepdims=True)
    return attend(tokens, weight, bias, spots, targets)[None]


def solution(mesh):
    placed = (
        P("fsdp", "seq", None),
        P("fsdp", "seq", None),
        P("fsdp"),
        P(None, "fsdp"),
        P(None, None, "seq"),
        P("fsdp", "seq"),
        P("fsdp", None),
        P("fsdp"),
    )
    return jax.shard_map(
        shards, mesh=mesh, in_specs=placed, out_specs=P("fsdp", None, "seq"), check_vma=False
    )
```

```python
import functools
import math

import jax
import jax.numpy as jnp
from jax import lax
from jax.experimental import pallas as pl
from jax.experimental.pallas import tpu as pltpu
from jax.sharding import PartitionSpec as P

HEAD_DIM = 64
FREQ = 256
SLOTS = 32
MIB = 1024 * 1024
F32 = jnp.float32
BF16 = jnp.bfloat16


def embed_times(stamps):
    half = FREQ // 2
    steps = jnp.arange(half, dtype=F32)
    freqs = jnp.exp(-math.log(10000.0) * steps / half)
    angles = stamps.astype(F32)[:, None] * freqs[None, :]
    raw = jnp.concatenate([jnp.cos(angles), jnp.sin(angles)], axis=1)
    return jax.nn.silu(raw).astype(BF16)


def norm_kernel(stamp_ref, latents_ref, noise_ref, out_ref):
    sigma = stamp_ref[0].astype(F32) / 1000.0
    noised = (1.0 - sigma) * latents_ref[...].astype(F32) + sigma * noise_ref[...].astype(F32)
    center = jnp.mean(noised, axis=1, keepdims=True)
    shifted = noised - center
    spread = jnp.mean(shifted * shifted, axis=1, keepdims=True)
    out_ref[...] = (shifted * lax.rsqrt(spread + 1e-06)).astype(BF16)


def normalize(timesteps, latents, noise):
    rows, dmodel = latents.shape
    block = 64
    spec = pl.BlockSpec((block, dmodel), lambda i: (i, 0))
    return pl.pallas_call(
        norm_kernel,
        grid=(rows // block,),
        in_specs=[pl.BlockSpec(memory_space=pltpu.SMEM), spec, spec],
        out_specs=spec,
        out_shape=jax.ShapeDtypeStruct((rows, dmodel), BF16),
        compiler_params=pltpu.CompilerParams(vmem_limit_bytes=16 * MIB),
        name="normalize",
    )(timesteps, latents, noise)


def onehot(mask):
    return mask.astype(F32).astype(BF16)


def pack_kernel(stamp_ref, owner_ref, place_ref, target_ref, out_ref):
    samples = out_ref.shape[0]
    crows, width = target_ref.shape
    owners = owner_ref[...]
    places = place_ref[...]
    owned = onehot(lax.broadcasted_iota(jnp.int32, (samples, crows), 0) == owners)
    earlier = onehot(
        lax.broadcasted_iota(jnp.int32, (crows, crows), 0)
        < lax.broadcasted_iota(jnp.int32, (crows, crows), 1)
    )
    before = jnp.dot(owned, earlier, preferred_element_type=F32)
    rank = jnp.sum(before * owned.astype(F32), axis=0, keepdims=True).astype(jnp.int32)
    slot = owners * SLOTS + rank
    select = onehot(lax.broadcasted_iota(jnp.int32, (samples * SLOTS, crows), 0) == slot)
    rows = jnp.dot(select, target_ref[...], preferred_element_type=F32).astype(BF16)
    out_ref[:, :SLOTS, :] = rows.reshape(samples, SLOTS, width)
    line = lax.broadcasted_iota(jnp.int32, (width, crows), 0)
    high = (lax.shift_right_logical(places, 6) + 1).astype(F32)
    low = (places & 63).astype(F32)
    coded = jnp.where(line == rank, high, jnp.where(line == rank + SLOTS, low, 0.0)).astype(BF16)
    extra = lax.dot_general(owned, coded, (((1,), (1,)), ((), ())), preferred_element_type=F32)
    lane = lax.broadcasted_iota(jnp.int32, (samples, width), 1)
    stamp = stamp_ref[0]
    upper = lax.shift_right_logical(stamp, 5).astype(F32)
    lower = (stamp & 31).astype(F32)
    extra = jnp.where(lane == 2 * SLOTS, upper, jnp.where(lane == 2 * SLOTS + 1, lower, extra))
    out_ref[:, SLOTS:, :] = jnp.broadcast_to(extra.astype(BF16)[:, None, :], (samples, 16, width))


def pack_rows(timesteps, owners, places, targets, samples):
    vmem = pl.BlockSpec(memory_space=pltpu.VMEM)
    return pl.pallas_call(
        pack_kernel,
        in_specs=[pl.BlockSpec(memory_space=pltpu.SMEM), vmem, vmem, vmem],
        out_specs=vmem,
        out_shape=jax.ShapeDtypeStruct((samples, SLOTS + 16, targets.shape[1]), BF16),
        compiler_params=pltpu.CompilerParams(vmem_limit_bytes=16 * MIB),
        name="pack_rows",
    )(timesteps, owners, places, targets)


def weight_kernel(scale_ref, shift_ref, own_ref, other_ref, out_ref, bias_ref):
    parts, _, width = own_ref.shape
    gain = 1.0 + scale_ref[...]
    shift = jnp.broadcast_to(shift_ref[...], (8, shift_ref.shape[1]))
    high = shift.astype(BF16)
    low = (shift - high.astype(F32)).astype(BF16)
    for part in range(2 * parts):
        weight = own_ref[part] if part < parts else other_ref[part - parts]
        span = slice(part * width, (part + 1) * width)
        out_ref[:, span] = (gain * weight.astype(F32)).astype(BF16)
        total = jnp.dot(high, weight, preferred_element_type=F32)
        total += jnp.dot(low, weight, preferred_element_type=F32)
        bias_ref[:, span] = total[:1]


def fold_weight(scale, shift, own, other):
    parts, dmodel, width = own.shape
    vmem = pl.BlockSpec(memory_space=pltpu.VMEM)
    return pl.pallas_call(
        weight_kernel,
        in_specs=[vmem] * 4,
        out_specs=[vmem] * 2,
        out_shape=[
            jax.ShapeDtypeStruct((dmodel, 2 * parts * width), BF16),
            jax.ShapeDtypeStruct((1, 2 * parts * width), F32),
        ],
        compiler_params=pltpu.CompilerParams(vmem_limit_bytes=20 * MIB),
        name="fold_weight",
    )(scale.reshape(dmodel, 1), shift.reshape(1, dmodel), own, other)


def project_kernel(count, *refs):
    weight_ref, bias_ref, column_ref, spot_ref, other_spot_ref, got_ref = refs[:6]
    token_refs, (pair_ref, send_ref, query_ref) = refs[6 : 6 + count], refs[6 + count :]
    width = query_ref.shape[1]
    base = 0
    total = jnp.zeros(query_ref.shape, F32)
    for token_ref in token_refs:
        here = slice(base, base + token_ref.shape[0])
        base += token_ref.shape[0]
        qkv = jnp.dot(token_ref[...], weight_ref[...], preferred_element_type=F32) + bias_ref[...]
        qkv = qkv.astype(BF16)
        pair_ref[here, :] = qkv[:, width : 3 * width]
        send_ref[here, :] = qkv[:, 3 * width :]
        pick = onehot(column_ref[...] == spot_ref[:, here])
        total += jnp.dot(pick, qkv[:, :width], preferred_element_type=F32)
    pick = onehot(column_ref[...] == other_spot_ref[...])
    total += jnp.dot(pick, got_ref[:, :width], preferred_element_type=F32)
    query_ref[...] = total.astype(BF16)


def first_kernel(count, *refs):
    weight_ref, bias_ref, column_ref, spot_ref = refs[:4]
    token_refs, (pair_ref, send_ref, query_ref) = refs[4 : 4 + count], refs[4 + count :]
    width = query_ref.shape[1]
    base = 0
    total = jnp.zeros(query_ref.shape, F32)
    for token_ref in token_refs:
        here = slice(base, base + token_ref.shape[0])
        base += token_ref.shape[0]
        qkv = jnp.dot(token_ref[...], weight_ref[...], preferred_element_type=F32) + bias_ref[...]
        qkv = qkv.astype(BF16)
        pair_ref[here, :] = qkv[:, width : 3 * width]
        send_ref[here, :] = qkv[:, 3 * width :]
        pick = onehot(column_ref[...] == spot_ref[:, here])
        total += jnp.dot(pick, qkv[:, :width], preferred_element_type=F32)
    query_ref[...] = total.astype(BF16)


def project(weight, bias, column, spots, tokens, received=()):
    rows = sum(block.shape[0] for block in tokens)
    width = weight.shape[1] // 6
    vmem = pl.BlockSpec(memory_space=pltpu.VMEM)
    body = project_kernel if received else first_kernel
    return pl.pallas_call(
        functools.partial(body, len(tokens)),
        in_specs=[vmem] * (4 + len(received) + len(tokens)),
        out_specs=[vmem] * 3,
        out_shape=[
            jax.ShapeDtypeStruct((rows, 2 * width), BF16),
            jax.ShapeDtypeStruct((rows, 3 * width), BF16),
            jax.ShapeDtypeStruct((column.shape[0], width), BF16),
        ],
        compiler_params=pltpu.CompilerParams(vmem_limit_bytes=20 * MIB),
        cost_estimate=pl.CostEstimate(
            flops=4 * rows * weight.size, bytes_accessed=8 * MIB, transcendentals=0
        ),
        name="project",
    )(weight, bias, column, spots, *received, *tokens)


def attend_kernel(count, column_ref, row_ref, spot_ref, target_ref, *refs):
    pair_refs, got_refs, query_refs = refs[:count], refs[count : 2 * count], refs[2 * count : 3 * count]
    out_ref, key_ref, first_ref, second_ref, query_ref, diff_ref = refs[3 * count :]
    slots, width = query_ref.shape
    length = key_ref.shape[0]
    base = 0
    for block_ref in (*pair_refs, *got_refs):
        here = slice(base, base + block_ref.shape[0])
        base += block_ref.shape[0]
        skip = block_ref.shape[1] - 2 * width
        value = block_ref[:, skip + width :]
        left = lax.broadcasted_iota(jnp.int32, value.shape, 1) < HEAD_DIM
        one = jnp.ones(value.shape, BF16)
        key_ref[here, :] = block_ref[:, skip : skip + width]
        first_ref[here, :] = jnp.where(left, value, one)
        second_ref[here, :] = jnp.where(left, one, value)
    query = sum(part[...].astype(F32) for part in query_refs)
    pick = onehot(column_ref[...] == spot_ref[...])
    query += jnp.dot(pick, got_refs[-1][:, :width], preferred_element_type=F32)
    query_ref[...] = query
    factor = math.log2(math.e) / math.sqrt(HEAD_DIM)
    part = 256
    half = lax.broadcasted_iota(jnp.int32, (part, width), 1) < HEAD_DIM
    for start in range(0, slots, part):
        query = query_ref[start : start + part, :]
        outs = []
        for mask, value_ref in ((half, first_ref), (~half, second_ref)):
            mine = jnp.where(mask, query, 0.0).astype(BF16)
            scores = lax.dot_general(
                mine, key_ref[...], (((1,), (1,)), ((), ())), preferred_element_type=F32
            )
            top = jnp.max(scores, axis=1, keepdims=True)
            probs = jnp.exp2((scores - top) * factor).astype(BF16)
            mixed = jnp.dot(probs, value_ref[...], preferred_element_type=F32)
            outs.append(mixed / pltpu.roll(mixed, HEAD_DIM, 1))
        attended = jnp.where(half, outs[0], outs[1])
        target = target_ref[start : start + part, :].astype(F32)
        diff_ref[start : start + part, :] = (attended - target).astype(BF16)
    for start in range(0, length, part):
        spots = lax.broadcasted_iota(jnp.int32, (part, slots), 0) + start
        spread = onehot(row_ref[...] == spots)
        out_ref[start : start + part, :] = jnp.dot(
            spread, diff_ref[...], preferred_element_type=F32
        ).astype(BF16)


def attend(column, row, spots, targets, pairs, received, queries):
    slots, width = targets.shape
    length = sum(block.shape[0] for block in (*pairs, *received))
    vmem = pl.BlockSpec(memory_space=pltpu.VMEM)
    return pl.pallas_call(
        functools.partial(attend_kernel, len(pairs)),
        in_specs=[vmem] * (4 + 3 * len(pairs)),
        out_specs=vmem,
        out_shape=jax.ShapeDtypeStruct((length, width), BF16),
        scratch_shapes=[
            pltpu.VMEM((length, width), BF16),
            pltpu.VMEM((length, width), BF16),
            pltpu.VMEM((length, width), BF16),
            pltpu.VMEM((slots, width), F32),
            pltpu.VMEM((slots, width), BF16),
        ],
        compiler_params=pltpu.CompilerParams(vmem_limit_bytes=28 * MIB),
        name="attend",
    )(column, row, spots, targets, *pairs, *received, *queries)


def after(array, *earlier):
    return lax.optimization_barrier((array, earlier))[0]


def shards(
    latents, noise, timesteps, time_weight, qkv_weight, cached_targets, cache_owner, cache_pos
):
    dmodel = latents.shape[2]
    own = latents.shape[1]
    width = qkv_weight.shape[2]
    samples = lax.axis_size("fsdp")
    group = lax.axis_size("seq")
    crows = cached_targets.shape[0]
    me = lax.axis_index("seq")
    swap = [(i, i ^ 1) for i in range(group)]
    onward = [(i, (i + 2 - 4 * (i % 2)) % group) for i in range(group)]
    backward = [(i, (i - 2 + 4 * (i % 2)) % group) for i in range(group)]

    def spots_of(device, hop):
        origin = jnp.where(device % 2 == 0, device - 2 * hop, device + 2 * hop) % group
        return own * origin + jnp.arange(own, dtype=jnp.int32)

    def group_spots(device, hop_list):
        return jnp.concatenate([spots_of(device, hop) for hop in hop_list])[None, :]

    normed = normalize(timesteps, latents[0], noise[0])
    up1 = lax.ppermute(normed, "seq", onward)
    down1 = lax.ppermute(normed, "seq", backward)
    sent = pack_rows(
        timesteps, cache_owner.reshape(1, crows), cache_pos.reshape(1, crows), cached_targets, samples
    )
    got = lax.all_to_all(after(sent, normed), "fsdp", 0, 0, tiled=True)
    raw = qkv_weight.transpose(1, 0, 2)
    other_raw = lax.ppermute(after(raw, normed), "seq", swap)
    up2 = lax.ppermute(up1, "seq", onward)
    down2 = lax.ppermute(down1, "seq", backward)

    targets = got[:, :SLOTS].reshape(samples * SLOTS, width)
    extra = got[:, SLOTS].astype(F32)
    high, low = extra[:, :SLOTS], extra[:, SLOTS : 2 * SLOTS]
    places = jnp.where(high > 0.5, (high - 1.0) * 64.0 + low, -1.0).astype(jnp.int32)
    column = places.reshape(samples * SLOTS, 1)
    row = places.reshape(1, samples * SLOTS)
    stamps = (extra[:, 2 * SLOTS] * 32.0 + extra[:, 2 * SLOTS + 1]).astype(jnp.int32)
    part = jnp.dot(embed_times(stamps), time_weight, preferred_element_type=F32)
    up3 = lax.ppermute(up2, "seq", onward)
    modulation = lax.all_to_all(after(part, up1), "fsdp", 0, 0, tiled=True).reshape(2 * dmodel)
    down3 = lax.ppermute(after(down2, part), "seq", backward)
    weight, bias = fold_weight(modulation[dmodel:], modulation[:dmodel], raw, other_raw)

    hops = ([0, 1, -1, 2, -2], [3, -3], [4])
    spots = [group_spots(me, hop_list) for hop_list in hops]
    other_spots = [group_spots(me ^ 1, hop_list) for hop_list in hops]
    first = project(weight, bias, column, spots[0], [normed, up1, down1, up2, down2])
    got_first = lax.ppermute(first[1], "seq", swap)
    up4 = lax.ppermute(after(up3, *first), "seq", onward)
    second = project(
        weight, bias, column, spots[1], [up3, down3], (other_spots[0], got_first)
    )
    got_second = lax.ppermute(second[1], "seq", swap)
    third = project(weight, bias, column, spots[2], [up4], (other_spots[1], got_second))
    got_third = lax.ppermute(third[1], "seq", swap)
    pairs, _, queries = zip(first, second, third)
    received = (got_first, got_second, got_third)
    return attend(column, row, other_spots[2], targets, pairs, received, queries)[None]


def solution(mesh):
    placed = (
        P("fsdp", "seq", None),
        P("fsdp", "seq", None),
        P("fsdp"),
        P(None, "fsdp"),
        P(None, None, "seq"),
        P("fsdp", "seq"),
        P("fsdp", None),
        P("fsdp"),
    )
    return jax.shard_map(
        shards, mesh=mesh, in_specs=placed, out_specs=P("fsdp", None, "seq"), check_vma=False
    )
```

```python
import functools
import math

import jax
import jax.numpy as jnp
from jax import lax
from jax.experimental import pallas as pl
from jax.experimental.pallas import tpu as pltpu
from jax.sharding import PartitionSpec as P

HEAD_DIM = 64
FREQ = 256
SLOTS = 32
MIB = 1024 * 1024
F32 = jnp.float32
BF16 = jnp.bfloat16


def embed_times(stamps):
    half = FREQ // 2
    steps = jnp.arange(half, dtype=F32)
    freqs = jnp.exp(-math.log(10000.0) * steps / half)
    angles = stamps.astype(F32)[:, None] * freqs[None, :]
    raw = jnp.concatenate([jnp.cos(angles), jnp.sin(angles)], axis=1)
    return jax.nn.silu(raw).astype(BF16)


def norm_kernel(stamp_ref, latents_ref, noise_ref, out_ref):
    sigma = stamp_ref[0].astype(F32) / 1000.0
    noised = (1.0 - sigma) * latents_ref[...].astype(F32) + sigma * noise_ref[...].astype(F32)
    center = jnp.mean(noised, axis=1, keepdims=True)
    shifted = noised - center
    spread = jnp.mean(shifted * shifted, axis=1, keepdims=True)
    out_ref[...] = (shifted * lax.rsqrt(spread + 1e-06)).astype(BF16)


def normalize(timesteps, latents, noise):
    rows, dmodel = latents.shape
    block = 64
    spec = pl.BlockSpec((block, dmodel), lambda i: (i, 0))
    return pl.pallas_call(
        norm_kernel,
        grid=(rows // block,),
        in_specs=[pl.BlockSpec(memory_space=pltpu.SMEM), spec, spec],
        out_specs=spec,
        out_shape=jax.ShapeDtypeStruct((rows, dmodel), BF16),
        compiler_params=pltpu.CompilerParams(vmem_limit_bytes=16 * MIB),
        name="normalize",
    )(timesteps, latents, noise)


def onehot(mask):
    return mask.astype(F32).astype(BF16)


def pack_kernel(stamp_ref, owner_ref, place_ref, target_ref, out_ref):
    samples = out_ref.shape[0]
    crows, width = target_ref.shape
    owners = owner_ref[...]
    places = place_ref[...]
    owned = onehot(lax.broadcasted_iota(jnp.int32, (samples, crows), 0) == owners)
    earlier = onehot(
        lax.broadcasted_iota(jnp.int32, (crows, crows), 0)
        < lax.broadcasted_iota(jnp.int32, (crows, crows), 1)
    )
    before = jnp.dot(owned, earlier, preferred_element_type=F32)
    rank = jnp.sum(before * owned.astype(F32), axis=0, keepdims=True).astype(jnp.int32)
    slot = owners * SLOTS + rank
    select = onehot(lax.broadcasted_iota(jnp.int32, (samples * SLOTS, crows), 0) == slot)
    rows = jnp.dot(select, target_ref[...], preferred_element_type=F32).astype(BF16)
    out_ref[:, :SLOTS, :] = rows.reshape(samples, SLOTS, width)
    line = lax.broadcasted_iota(jnp.int32, (width, crows), 0)
    high = (lax.shift_right_logical(places, 6) + 1).astype(F32)
    low = (places & 63).astype(F32)
    coded = jnp.where(line == rank, high, jnp.where(line == rank + SLOTS, low, 0.0)).astype(BF16)
    extra = lax.dot_general(owned, coded, (((1,), (1,)), ((), ())), preferred_element_type=F32)
    lane = lax.broadcasted_iota(jnp.int32, (samples, width), 1)
    stamp = stamp_ref[0]
    upper = lax.shift_right_logical(stamp, 5).astype(F32)
    lower = (stamp & 31).astype(F32)
    extra = jnp.where(lane == 2 * SLOTS, upper, jnp.where(lane == 2 * SLOTS + 1, lower, extra))
    out_ref[:, SLOTS:, :] = jnp.broadcast_to(extra.astype(BF16)[:, None, :], (samples, 16, width))


def pack_rows(timesteps, owners, places, targets, samples):
    vmem = pl.BlockSpec(memory_space=pltpu.VMEM)
    return pl.pallas_call(
        pack_kernel,
        in_specs=[pl.BlockSpec(memory_space=pltpu.SMEM), vmem, vmem, vmem],
        out_specs=vmem,
        out_shape=jax.ShapeDtypeStruct((samples, SLOTS + 16, targets.shape[1]), BF16),
        compiler_params=pltpu.CompilerParams(vmem_limit_bytes=16 * MIB),
        name="pack_rows",
    )(timesteps, owners, places, targets)


def weight_kernel(scale_ref, shift_ref, own_ref, other_ref, out_ref, bias_ref):
    parts, _, width = own_ref.shape
    gain = 1.0 + scale_ref[...]
    shift = jnp.broadcast_to(shift_ref[...], (8, shift_ref.shape[1]))
    high = shift.astype(BF16)
    low = (shift - high.astype(F32)).astype(BF16)
    both = jnp.concatenate([high, low], axis=0)
    for part in range(2 * parts):
        weight = own_ref[part] if part < parts else other_ref[part - parts]
        span = slice(part * width, (part + 1) * width)
        out_ref[:, span] = (gain * weight.astype(F32)).astype(BF16)
        total = jnp.dot(both, weight, preferred_element_type=F32)
        bias_ref[:, span] = total[:1] + total[8:9]


def fold_weight(scale, shift, own, other):
    parts, dmodel, width = own.shape
    vmem = pl.BlockSpec(memory_space=pltpu.VMEM)
    return pl.pallas_call(
        weight_kernel,
        in_specs=[vmem] * 4,
        out_specs=[vmem] * 2,
        out_shape=[
            jax.ShapeDtypeStruct((dmodel, 2 * parts * width), BF16),
            jax.ShapeDtypeStruct((1, 2 * parts * width), F32),
        ],
        compiler_params=pltpu.CompilerParams(vmem_limit_bytes=14 * MIB),
        name="fold_weight",
    )(scale.reshape(dmodel, 1), shift.reshape(1, dmodel), own, other)


def project_kernel(count, *refs):
    weight_ref, bias_ref, column_ref, spot_ref, other_spot_ref, got_ref = refs[:6]
    token_refs, (pair_ref, send_ref, query_ref) = refs[6 : 6 + count], refs[6 + count :]
    width = query_ref.shape[1]
    tokens = jnp.concatenate([token_ref[...] for token_ref in token_refs], axis=0)
    qkv = jnp.dot(tokens, weight_ref[...], preferred_element_type=F32) + bias_ref[...]
    qkv = qkv.astype(BF16)
    pair_ref[...] = qkv[:, width : 3 * width]
    send_ref[...] = qkv[:, 3 * width :]
    pick = onehot(column_ref[...] == spot_ref[...])
    total = jnp.dot(pick, qkv[:, :width], preferred_element_type=F32)
    pick = onehot(column_ref[...] == other_spot_ref[...])
    total += jnp.dot(pick, got_ref[:, :width], preferred_element_type=F32)
    query_ref[...] = total.astype(BF16)


def first_kernel(count, *refs):
    weight_ref, bias_ref, column_ref, spot_ref = refs[:4]
    token_refs, (pair_ref, send_ref, query_ref) = refs[4 : 4 + count], refs[4 + count :]
    width = query_ref.shape[1]
    tokens = jnp.concatenate([token_ref[...] for token_ref in token_refs], axis=0)
    qkv = jnp.dot(tokens, weight_ref[...], preferred_element_type=F32) + bias_ref[...]
    qkv = qkv.astype(BF16)
    pair_ref[...] = qkv[:, width : 3 * width]
    send_ref[...] = qkv[:, 3 * width :]
    pick = onehot(column_ref[...] == spot_ref[...])
    total = jnp.dot(pick, qkv[:, :width], preferred_element_type=F32)
    query_ref[...] = total.astype(BF16)


def project(weight, bias, column, spots, tokens, received=()):
    rows = sum(block.shape[0] for block in tokens)
    width = weight.shape[1] // 6
    vmem = pl.BlockSpec(memory_space=pltpu.VMEM)
    body = project_kernel if received else first_kernel
    return pl.pallas_call(
        functools.partial(body, len(tokens)),
        in_specs=[vmem] * (4 + len(received) + len(tokens)),
        out_specs=[vmem] * 3,
        out_shape=[
            jax.ShapeDtypeStruct((rows, 2 * width), BF16),
            jax.ShapeDtypeStruct((rows, 3 * width), BF16),
            jax.ShapeDtypeStruct((column.shape[0], width), BF16),
        ],
        compiler_params=pltpu.CompilerParams(vmem_limit_bytes=14 * MIB),
        cost_estimate=pl.CostEstimate(
            flops=4 * rows * weight.size, bytes_accessed=8 * MIB, transcendentals=0
        ),
        name="project",
    )(weight, bias, column, spots, *received, *tokens)


def attend_kernel(count, column_ref, row_ref, spot_ref, target_ref, *refs):
    pair_refs, got_refs, query_refs = refs[:count], refs[count : 2 * count], refs[2 * count : 3 * count]
    out_ref, key_ref, first_ref, second_ref, query_ref, diff_ref = refs[3 * count :]
    slots, width = query_ref.shape
    length = key_ref.shape[0]
    base = 0
    for block_ref in (*pair_refs, *got_refs):
        here = slice(base, base + block_ref.shape[0])
        base += block_ref.shape[0]
        skip = block_ref.shape[1] - 2 * width
        value = block_ref[:, skip + width :]
        left = lax.broadcasted_iota(jnp.int32, value.shape, 1) < HEAD_DIM
        one = jnp.ones(value.shape, BF16)
        key_ref[here, :] = block_ref[:, skip : skip + width]
        first_ref[here, :] = jnp.where(left, value, one)
        second_ref[here, :] = jnp.where(left, one, value)
    query = sum(part[...].astype(F32) for part in query_refs)
    pick = onehot(column_ref[...] == spot_ref[...])
    query += jnp.dot(pick, got_refs[-1][:, :width], preferred_element_type=F32)
    query_ref[...] = query
    factor = math.log2(math.e) / math.sqrt(HEAD_DIM)
    part = 256
    half = lax.broadcasted_iota(jnp.int32, (part, width), 1) < HEAD_DIM
    for start in range(0, slots, part):
        query = query_ref[start : start + part, :]
        outs = []
        for mask, value_ref in ((half, first_ref), (~half, second_ref)):
            mine = jnp.where(mask, query, 0.0).astype(BF16)
            scores = lax.dot_general(
                mine, key_ref[...], (((1,), (1,)), ((), ())), preferred_element_type=F32
            )
            top = jnp.max(scores, axis=1, keepdims=True)
            probs = jnp.exp2((scores - top) * factor).astype(BF16)
            mixed = jnp.dot(probs, value_ref[...], preferred_element_type=F32)
            outs.append(mixed / pltpu.roll(mixed, HEAD_DIM, 1))
        attended = jnp.where(half, outs[0], outs[1])
        target = target_ref[start : start + part, :].astype(F32)
        diff_ref[start : start + part, :] = (attended - target).astype(BF16)
    for start in range(0, length, part):
        spots = lax.broadcasted_iota(jnp.int32, (part, slots), 0) + start
        spread = onehot(row_ref[...] == spots)
        out_ref[start : start + part, :] = jnp.dot(
            spread, diff_ref[...], preferred_element_type=F32
        ).astype(BF16)


def attend(column, row, spots, targets, pairs, received, queries):
    slots, width = targets.shape
    length = sum(block.shape[0] for block in (*pairs, *received))
    vmem = pl.BlockSpec(memory_space=pltpu.VMEM)
    return pl.pallas_call(
        functools.partial(attend_kernel, len(pairs)),
        in_specs=[vmem] * (4 + 3 * len(pairs)),
        out_specs=vmem,
        out_shape=jax.ShapeDtypeStruct((length, width), BF16),
        scratch_shapes=[
            pltpu.VMEM((length, width), BF16),
            pltpu.VMEM((length, width), BF16),
            pltpu.VMEM((length, width), BF16),
            pltpu.VMEM((slots, width), F32),
            pltpu.VMEM((slots, width), BF16),
        ],
        compiler_params=pltpu.CompilerParams(vmem_limit_bytes=20 * MIB),
        name="attend",
    )(column, row, spots, targets, *pairs, *received, *queries)


def after(array, *earlier):
    return lax.optimization_barrier((array, earlier))[0]


def shards(
    latents, noise, timesteps, time_weight, qkv_weight, cached_targets, cache_owner, cache_pos
):
    dmodel = latents.shape[2]
    own = latents.shape[1]
    width = qkv_weight.shape[2]
    samples = lax.axis_size("fsdp")
    group = lax.axis_size("seq")
    crows = cached_targets.shape[0]
    me = lax.axis_index("seq")
    swap = [(i, i ^ 1) for i in range(group)]
    onward = [(i, (i + 2 - 4 * (i % 2)) % group) for i in range(group)]
    backward = [(i, (i - 2 + 4 * (i % 2)) % group) for i in range(group)]

    def spots_of(device, hop):
        origin = jnp.where(device % 2 == 0, device - 2 * hop, device + 2 * hop) % group
        return own * origin + jnp.arange(own, dtype=jnp.int32)

    def group_spots(device, hop_list):
        return jnp.concatenate([spots_of(device, hop) for hop in hop_list])[None, :]

    normed = normalize(timesteps, latents[0], noise[0])
    up1 = lax.ppermute(normed, "seq", onward)
    down1 = lax.ppermute(normed, "seq", backward)
    sent = pack_rows(
        timesteps, cache_owner.reshape(1, crows), cache_pos.reshape(1, crows), cached_targets, samples
    )
    got = lax.all_to_all(after(sent, normed), "fsdp", 0, 0, tiled=True)
    raw = qkv_weight.transpose(1, 0, 2)
    other_raw = lax.ppermute(after(raw, normed), "seq", swap)
    up2 = lax.ppermute(up1, "seq", onward)
    down2 = lax.ppermute(down1, "seq", backward)

    targets = got[:, :SLOTS].reshape(samples * SLOTS, width)
    extra = got[:, SLOTS].astype(F32)
    high, low = extra[:, :SLOTS], extra[:, SLOTS : 2 * SLOTS]
    places = jnp.where(high > 0.5, (high - 1.0) * 64.0 + low, -1.0).astype(jnp.int32)
    column = places.reshape(samples * SLOTS, 1)
    row = places.reshape(1, samples * SLOTS)
    stamps = (extra[:, 2 * SLOTS] * 32.0 + extra[:, 2 * SLOTS + 1]).astype(jnp.int32)
    part = jnp.dot(embed_times(stamps), time_weight, preferred_element_type=F32)
    up3 = lax.ppermute(up2, "seq", onward)
    modulation = lax.all_to_all(after(part, up1), "fsdp", 0, 0, tiled=True).reshape(2 * dmodel)
    down3 = lax.ppermute(after(down2, part), "seq", backward)
    weight, bias = fold_weight(modulation[dmodel:], modulation[:dmodel], raw, other_raw)

    hops = ([0, 1, -1, 2, -2], [3, -3], [4])
    spots = [group_spots(me, hop_list) for hop_list in hops]
    other_spots = [group_spots(me ^ 1, hop_list) for hop_list in hops]
    first = project(weight, bias, column, spots[0], [normed, up1, down1, up2, down2])
    got_first = lax.ppermute(first[1], "seq", swap)
    up4 = lax.ppermute(after(up3, *first), "seq", onward)
    second = project(
        weight, bias, column, spots[1], [up3, down3], (other_spots[0], got_first)
    )
    got_second = lax.ppermute(second[1], "seq", swap)
    third = project(weight, bias, column, spots[2], [up4], (other_spots[1], got_second))
    got_third = lax.ppermute(third[1], "seq", swap)
    pairs, _, queries = zip(first, second, third)
    received = (got_first, got_second, got_third)
    return attend(column, row, other_spots[2], targets, pairs, received, queries)[None]


def solution(mesh):
    placed = (
        P("fsdp", "seq", None),
        P("fsdp", "seq", None),
        P("fsdp"),
        P(None, "fsdp"),
        P(None, None, "seq"),
        P("fsdp", "seq"),
        P("fsdp", None),
        P("fsdp"),
    )
    return jax.shard_map(
        shards, mesh=mesh, in_specs=placed, out_specs=P("fsdp", None, "seq"), check_vma=False
    )
```

```python
import functools
import math

import jax
import jax.numpy as jnp
from jax import lax
from jax.experimental import pallas as pl
from jax.experimental.pallas import tpu as pltpu
from jax.sharding import PartitionSpec as P

HEAD_DIM = 64
FREQ = 256
SLOTS = 32
MIB = 1024 * 1024
F32 = jnp.float32
BF16 = jnp.bfloat16


def embed_times(stamps):
    half = FREQ // 2
    steps = jnp.arange(half, dtype=F32)
    freqs = jnp.exp(-math.log(10000.0) * steps / half)
    angles = stamps.astype(F32)[:, None] * freqs[None, :]
    raw = jnp.concatenate([jnp.cos(angles), jnp.sin(angles)], axis=1)
    return jax.nn.silu(raw).astype(BF16)


def norm_kernel(stamp_ref, latents_ref, noise_ref, out_ref):
    sigma = stamp_ref[0].astype(F32) / 1000.0
    noised = (1.0 - sigma) * latents_ref[...].astype(F32) + sigma * noise_ref[...].astype(F32)
    center = jnp.mean(noised, axis=1, keepdims=True)
    shifted = noised - center
    spread = jnp.mean(shifted * shifted, axis=1, keepdims=True)
    out_ref[...] = (shifted * lax.rsqrt(spread + 1e-06)).astype(BF16)


def normalize(timesteps, latents, noise):
    rows, dmodel = latents.shape
    block = 64
    spec = pl.BlockSpec((block, dmodel), lambda i: (i, 0))
    return pl.pallas_call(
        norm_kernel,
        grid=(rows // block,),
        in_specs=[pl.BlockSpec(memory_space=pltpu.SMEM), spec, spec],
        out_specs=spec,
        out_shape=jax.ShapeDtypeStruct((rows, dmodel), BF16),
        compiler_params=pltpu.CompilerParams(vmem_limit_bytes=16 * MIB),
        name="normalize",
    )(timesteps, latents, noise)


def onehot(mask):
    return mask.astype(F32).astype(BF16)


def pack_kernel(stamp_ref, owner_ref, place_ref, target_ref, out_ref):
    samples = out_ref.shape[0]
    crows, width = target_ref.shape
    owners = owner_ref[...]
    places = place_ref[...]
    owned = onehot(lax.broadcasted_iota(jnp.int32, (samples, crows), 0) == owners)
    earlier = onehot(
        lax.broadcasted_iota(jnp.int32, (crows, crows), 0)
        < lax.broadcasted_iota(jnp.int32, (crows, crows), 1)
    )
    before = jnp.dot(owned, earlier, preferred_element_type=F32)
    rank = jnp.sum(before * owned.astype(F32), axis=0, keepdims=True).astype(jnp.int32)
    slot = owners * SLOTS + rank
    select = onehot(lax.broadcasted_iota(jnp.int32, (samples * SLOTS, crows), 0) == slot)
    rows = jnp.dot(select, target_ref[...], preferred_element_type=F32).astype(BF16)
    out_ref[:, :SLOTS, :] = rows.reshape(samples, SLOTS, width)
    line = lax.broadcasted_iota(jnp.int32, (width, crows), 0)
    high = (lax.shift_right_logical(places, 6) + 1).astype(F32)
    low = (places & 63).astype(F32)
    coded = jnp.where(line == rank, high, jnp.where(line == rank + SLOTS, low, 0.0)).astype(BF16)
    extra = lax.dot_general(owned, coded, (((1,), (1,)), ((), ())), preferred_element_type=F32)
    lane = lax.broadcasted_iota(jnp.int32, (samples, width), 1)
    stamp = stamp_ref[0]
    upper = lax.shift_right_logical(stamp, 5).astype(F32)
    lower = (stamp & 31).astype(F32)
    extra = jnp.where(lane == 2 * SLOTS, upper, jnp.where(lane == 2 * SLOTS + 1, lower, extra))
    out_ref[:, SLOTS:, :] = jnp.broadcast_to(extra.astype(BF16)[:, None, :], (samples, 16, width))


def pack_rows(timesteps, owners, places, targets, samples):
    vmem = pl.BlockSpec(memory_space=pltpu.VMEM)
    return pl.pallas_call(
        pack_kernel,
        in_specs=[pl.BlockSpec(memory_space=pltpu.SMEM), vmem, vmem, vmem],
        out_specs=vmem,
        out_shape=jax.ShapeDtypeStruct((samples, SLOTS + 16, targets.shape[1]), BF16),
        compiler_params=pltpu.CompilerParams(vmem_limit_bytes=16 * MIB),
        name="pack_rows",
    )(timesteps, owners, places, targets)


def weight_kernel(scale_ref, shift_ref, own_ref, other_ref, out_ref, bias_ref):
    parts, _, width = own_ref.shape
    gain = 1.0 + scale_ref[...]
    shift = jnp.broadcast_to(shift_ref[...], (8, shift_ref.shape[1]))
    high = shift.astype(BF16)
    low = (shift - high.astype(F32)).astype(BF16)
    both = jnp.concatenate([high, low], axis=0)
    for part in range(2 * parts):
        weight = own_ref[part] if part < parts else other_ref[part - parts]
        span = slice(part * width, (part + 1) * width)
        out_ref[:, span] = (gain * weight.astype(F32)).astype(BF16)
        total = jnp.dot(both, weight, preferred_element_type=F32)
        bias_ref[:, span] = total[:1] + total[8:9]


def fold_weight(scale, shift, own, other):
    parts, dmodel, width = own.shape
    vmem = pl.BlockSpec(memory_space=pltpu.VMEM)
    return pl.pallas_call(
        weight_kernel,
        in_specs=[vmem] * 4,
        out_specs=[vmem] * 2,
        out_shape=[
            jax.ShapeDtypeStruct((dmodel, 2 * parts * width), BF16),
            jax.ShapeDtypeStruct((1, 2 * parts * width), F32),
        ],
        compiler_params=pltpu.CompilerParams(vmem_limit_bytes=14 * MIB),
        name="fold_weight",
    )(scale.reshape(dmodel, 1), shift.reshape(1, dmodel), own, other)


def project_kernel(count, *refs):
    weight_ref, bias_ref, column_ref, spot_ref, other_spot_ref, got_ref = refs[:6]
    token_refs, (pair_ref, send_ref, query_ref) = refs[6 : 6 + count], refs[6 + count :]
    width = query_ref.shape[1]
    tokens = jnp.concatenate([token_ref[...] for token_ref in token_refs], axis=0)
    qkv = jnp.dot(tokens, weight_ref[...], preferred_element_type=F32) + bias_ref[...]
    qkv = qkv.astype(BF16)
    pair_ref[...] = qkv[:, width : 3 * width]
    send_ref[...] = qkv[:, 3 * width :]
    pick = onehot(column_ref[...] == spot_ref[...])
    total = jnp.dot(pick, qkv[:, :width], preferred_element_type=F32)
    pick = onehot(column_ref[...] == other_spot_ref[...])
    total += jnp.dot(pick, got_ref[:, :width], preferred_element_type=F32)
    query_ref[...] = total.astype(BF16)


def first_kernel(count, *refs):
    weight_ref, bias_ref, column_ref, spot_ref = refs[:4]
    token_refs, (pair_ref, send_ref, query_ref) = refs[4 : 4 + count], refs[4 + count :]
    width = query_ref.shape[1]
    tokens = jnp.concatenate([token_ref[...] for token_ref in token_refs], axis=0)
    qkv = jnp.dot(tokens, weight_ref[...], preferred_element_type=F32) + bias_ref[...]
    qkv = qkv.astype(BF16)
    pair_ref[...] = qkv[:, width : 3 * width]
    send_ref[...] = qkv[:, 3 * width :]
    pick = onehot(column_ref[...] == spot_ref[...])
    total = jnp.dot(pick, qkv[:, :width], preferred_element_type=F32)
    query_ref[...] = total.astype(BF16)


def project(weight, bias, column, spots, tokens, received=()):
    rows = sum(block.shape[0] for block in tokens)
    width = weight.shape[1] // 6
    vmem = pl.BlockSpec(memory_space=pltpu.VMEM)
    body = project_kernel if received else first_kernel
    return pl.pallas_call(
        functools.partial(body, len(tokens)),
        in_specs=[vmem] * (4 + len(received) + len(tokens)),
        out_specs=[vmem] * 3,
        out_shape=[
            jax.ShapeDtypeStruct((rows, 2 * width), BF16),
            jax.ShapeDtypeStruct((rows, 3 * width), BF16),
            jax.ShapeDtypeStruct((column.shape[0], width), BF16),
        ],
        compiler_params=pltpu.CompilerParams(vmem_limit_bytes=14 * MIB),
        cost_estimate=pl.CostEstimate(
            flops=4 * rows * weight.size, bytes_accessed=8 * MIB, transcendentals=0
        ),
        name="project",
    )(weight, bias, column, spots, *received, *tokens)


def attend_kernel(count, column_ref, row_ref, spot_ref, target_ref, *refs):
    pair_refs, got_refs, query_refs = refs[:count], refs[count : 2 * count], refs[2 * count : 3 * count]
    out_ref, key_ref, first_ref, second_ref, query_ref, diff_ref = refs[3 * count :]
    slots, width = query_ref.shape
    length = key_ref.shape[0]
    base = 0
    for block_ref in (*pair_refs, *got_refs):
        here = slice(base, base + block_ref.shape[0])
        base += block_ref.shape[0]
        skip = block_ref.shape[1] - 2 * width
        value = block_ref[:, skip + width :]
        left = lax.broadcasted_iota(jnp.int32, value.shape, 1) < HEAD_DIM
        one = jnp.ones(value.shape, BF16)
        key_ref[here, :] = block_ref[:, skip : skip + width]
        first_ref[here, :] = jnp.where(left, value, one)
        second_ref[here, :] = jnp.where(left, one, value)
    query = sum(part[...].astype(F32) for part in query_refs)
    pick = onehot(column_ref[...] == spot_ref[...])
    query += jnp.dot(pick, got_refs[-1][:, :width], preferred_element_type=F32)
    query_ref[...] = query
    factor = math.log2(math.e) / math.sqrt(HEAD_DIM)
    part = 512
    half = lax.broadcasted_iota(jnp.int32, (part, width), 1) < HEAD_DIM
    for start in range(0, slots, part):
        query = query_ref[start : start + part, :]
        outs = []
        for mask, value_ref in ((half, first_ref), (~half, second_ref)):
            mine = jnp.where(mask, query, 0.0).astype(BF16)
            scores = lax.dot_general(
                mine, key_ref[...], (((1,), (1,)), ((), ())), preferred_element_type=F32
            )
            top = jnp.max(scores, axis=1, keepdims=True)
            probs = jnp.exp2((scores - top) * factor).astype(BF16)
            mixed = jnp.dot(probs, value_ref[...], preferred_element_type=F32)
            outs.append(mixed / pltpu.roll(mixed, HEAD_DIM, 1))
        attended = jnp.where(half, outs[0], outs[1])
        target = target_ref[start : start + part, :].astype(F32)
        diff_ref[start : start + part, :] = (attended - target).astype(BF16)
    part = 256
    for start in range(0, length, part):
        spots = lax.broadcasted_iota(jnp.int32, (part, slots), 0) + start
        spread = onehot(row_ref[...] == spots)
        out_ref[start : start + part, :] = jnp.dot(
            spread, diff_ref[...], preferred_element_type=F32
        ).astype(BF16)


def attend(column, row, spots, targets, pairs, received, queries):
    slots, width = targets.shape
    length = sum(block.shape[0] for block in (*pairs, *received))
    vmem = pl.BlockSpec(memory_space=pltpu.VMEM)
    return pl.pallas_call(
        functools.partial(attend_kernel, len(pairs)),
        in_specs=[vmem] * (4 + 3 * len(pairs)),
        out_specs=vmem,
        out_shape=jax.ShapeDtypeStruct((length, width), BF16),
        scratch_shapes=[
            pltpu.VMEM((length, width), BF16),
            pltpu.VMEM((length, width), BF16),
            pltpu.VMEM((length, width), BF16),
            pltpu.VMEM((slots, width), F32),
            pltpu.VMEM((slots, width), BF16),
        ],
        compiler_params=pltpu.CompilerParams(vmem_limit_bytes=28 * MIB),
        name="attend",
    )(column, row, spots, targets, *pairs, *received, *queries)


def after(array, *earlier):
    return lax.optimization_barrier((array, earlier))[0]


def shards(
    latents, noise, timesteps, time_weight, qkv_weight, cached_targets, cache_owner, cache_pos
):
    dmodel = latents.shape[2]
    own = latents.shape[1]
    width = qkv_weight.shape[2]
    samples = lax.axis_size("fsdp")
    group = lax.axis_size("seq")
    crows = cached_targets.shape[0]
    me = lax.axis_index("seq")
    swap = [(i, i ^ 1) for i in range(group)]
    onward = [(i, (i + 2 - 4 * (i % 2)) % group) for i in range(group)]
    backward = [(i, (i - 2 + 4 * (i % 2)) % group) for i in range(group)]

    def spots_of(device, hop):
        origin = jnp.where(device % 2 == 0, device - 2 * hop, device + 2 * hop) % group
        return own * origin + jnp.arange(own, dtype=jnp.int32)

    def group_spots(device, hop_list):
        return jnp.concatenate([spots_of(device, hop) for hop in hop_list])[None, :]

    normed = normalize(timesteps, latents[0], noise[0])
    up1 = lax.ppermute(normed, "seq", onward)
    down1 = lax.ppermute(normed, "seq", backward)
    sent = pack_rows(
        timesteps, cache_owner.reshape(1, crows), cache_pos.reshape(1, crows), cached_targets, samples
    )
    got = lax.all_to_all(after(sent, normed), "fsdp", 0, 0, tiled=True)
    raw = qkv_weight.transpose(1, 0, 2)
    other_raw = lax.ppermute(after(raw, normed), "seq", swap)
    up2 = lax.ppermute(up1, "seq", onward)
    down2 = lax.ppermute(down1, "seq", backward)

    targets = got[:, :SLOTS].reshape(samples * SLOTS, width)
    extra = got[:, SLOTS].astype(F32)
    high, low = extra[:, :SLOTS], extra[:, SLOTS : 2 * SLOTS]
    places = jnp.where(high > 0.5, (high - 1.0) * 64.0 + low, -1.0).astype(jnp.int32)
    column = places.reshape(samples * SLOTS, 1)
    row = places.reshape(1, samples * SLOTS)
    stamps = (extra[:, 2 * SLOTS] * 32.0 + extra[:, 2 * SLOTS + 1]).astype(jnp.int32)
    part = jnp.dot(embed_times(stamps), time_weight, preferred_element_type=F32)
    up3 = lax.ppermute(up2, "seq", onward)
    modulation = lax.all_to_all(after(part, up1), "fsdp", 0, 0, tiled=True).reshape(2 * dmodel)
    down3 = lax.ppermute(after(down2, part), "seq", backward)
    weight, bias = fold_weight(modulation[dmodel:], modulation[:dmodel], raw, other_raw)

    hops = ([0, 1, -1, 2, -2], [3, -3], [4])
    spots = [group_spots(me, hop_list) for hop_list in hops]
    other_spots = [group_spots(me ^ 1, hop_list) for hop_list in hops]
    first = project(weight, bias, column, spots[0], [normed, up1, down1, up2, down2])
    got_first = lax.ppermute(first[1], "seq", swap)
    up4 = lax.ppermute(after(up3, *first), "seq", onward)
    second = project(
        weight, bias, column, spots[1], [up3, down3], (other_spots[0], got_first)
    )
    got_second = lax.ppermute(second[1], "seq", swap)
    third = project(weight, bias, column, spots[2], [up4], (other_spots[1], got_second))
    got_third = lax.ppermute(third[1], "seq", swap)
    pairs, _, queries = zip(first, second, third)
    received = (got_first, got_second, got_third)
    return attend(column, row, other_spots[2], targets, pairs, received, queries)[None]


def solution(mesh):
    placed = (
        P("fsdp", "seq", None),
        P("fsdp", "seq", None),
        P("fsdp"),
        P(None, "fsdp"),
        P(None, None, "seq"),
        P("fsdp", "seq"),
        P("fsdp", None),
        P("fsdp"),
    )
    return jax.shard_map(
        shards, mesh=mesh, in_specs=placed, out_specs=P("fsdp", None, "seq"), check_vma=False
    )
```
